128 devices in a mesh: blk: 16 (over y, z_lo, core), team: 8 (over z_hi, x).
Axes of the slice: x: 4, y: 4, z: 4 (z_hi: 2, z_lo: 2; z = z_hi * 2 + z_lo), core: 2. Of those that a mesh axis runs over, the one named last changes fastest.
Arguments:
- features: bfloat16 [32768, 128], P(('blk', 'team')), may hold values from -0.796875 to 0.796875
- left_vectors: bfloat16 [32768, 128], P(('blk', 'team')), may hold values from -0.8984375 to 0.8984375
- right_vectors: bfloat16 [32768, 128], P(('blk', 'team')), may hold values from -0.8984375 to 0.8984375
Outputs:
- feature_grad: float32 [32768, 128], P(('blk', 'team'))
The draws below stay inside these ranges and needn't reach their ends.
All inputs are finite; a program needn't handle non-finite values.
Results may differ from the reference program's by a relative error of at most 0.0039.
Values may be sent and summed in bfloat16 or wider, within the bound.
No kernel may reach another device: no remote copies, remote signals or barrier semaphores. Data moves between devices by JAX's collectives and lax.ppermute only.
A program may use at most 64 MiB of HBM per device.

```python
import jax
import jax.numpy as jnp
from jax import lax

FEAT = 128
VEC = 128
POINTS = 32768


def steps_of(own_key, dims, pieces, least, high):
    gain, own = 1.0, jax.random.fold_in(own_key, 6)
    for position, parts in pieces:
        draws = jnp.exp(jax.random.uniform(jax.random.fold_in(own, position), (parts,), jnp.float32, least / len(pieces), high / len(pieces)))
        gain = gain * jnp.repeat(draws, dims[position] // parts).reshape([-1 if axis == position else 1 for axis in range(len(dims))])
    return gain


def normal_values(rng, dims, scale, reach, shards=(), kind=jnp.bfloat16):
    factor_of = steps_of(rng, dims, shards, -0.22, 0.18) if shards else 1.0
    drawn = jax.random.normal(rng, dims, jnp.float32) * scale * factor_of
    return jnp.minimum(jnp.maximum(drawn, -reach), reach).astype(kind)


def setup_inputs(seed: int = 0) -> dict:
    splits = jax.random.split(jax.random.key(seed), 4)
    return {
        "features": normal_values(splits[0], (POINTS, FEAT), 0.1, 0.796875, ((0, 128),)),
        "left_vectors": normal_values(splits[1], (POINTS, VEC), 0.11, 0.8984375, ((0, 128),)),
        "right_vectors": normal_values(splits[2], (POINTS, VEC), 0.11, 0.8984375, ((0, 128),)),
    }


def pair_block(target_x, target_l, target_r, target_norm, source_x, source_l, source_r, source_norm):
    cross = jnp.dot(target_x, source_x.T, preferred_element_type=jnp.float32)
    dist_sq = target_norm[:, None] + source_norm[None, :] - 2.0 * cross
    radius = jnp.sqrt(jnp.maximum(dist_sq, 0.0))
    couple = jnp.dot(target_l, source_r.T, preferred_element_type=jnp.float32) + jnp.dot(target_r, source_l.T, preferred_element_type=jnp.float32)
    root_five = jnp.float32(5.0) ** 0.5
    weight = (-(5.0 / 3.0) * (1.0 + root_five * radius) * jnp.exp(-root_five * radius) * couple).astype(jnp.bfloat16)
    row_total = lax.optimization_barrier(jnp.sum(weight.astype(jnp.float32), axis=1))
    return row_total[:, None] * target_x.astype(jnp.float32) - jnp.dot(weight, source_x, preferred_element_type=jnp.float32)

def reference(features, left_vectors, right_vectors):
    total = features.shape[0]
    width = min(512, total)
    norms = lax.optimization_barrier(jnp.sum(features.astype(jnp.float32) ** 2, axis=1))
    count_blocks = total // width

    def one_block(packed):
        block_x, block_l, block_r, block_norm = packed
        return pair_block(block_x, block_l, block_r, block_norm, features, left_vectors, right_vectors, norms)
    result = lax.map(one_block, (features.reshape(count_blocks, width, -1), left_vectors.reshape(count_blocks, width, -1), right_vectors.reshape(count_blocks, width, -1), norms.reshape(count_blocks, width)))
    return result.reshape(total, -1)
```

```python
import functools
import itertools
import math

import jax
import jax.numpy as jnp
import numpy as np
from jax import lax
from jax.experimental import pallas as pl
from jax.experimental.pallas import tpu as pltpu
from jax.sharding import PartitionSpec as P

MEMBERS = (
    ((0, 0, 0), (2, 3, 2), (3, 3, 0), (0, 0, 1), (1, 1, 3), (2, 0, 0), (0, 1, 0), (0, 3, 0)),
    ((0, 0, 0), (1, 0, 3), (0, 0, 2), (0, 3, 1), (1, 2, 0), (3, 1, 0), (0, 2, 0), (3, 0, 0)),
)
BOTH = (
    ((1, 0), (1, 2), (2, 0), (0, 3), (2, 3), (1, 3), (3, 4), (0, 4), (4, 1), (4, 2), (1, 5), (4, 5), (5, 3)),
    ((0, 1), (2, 1), (3, 2), (3, 0), (1, 4), (0, 4), (2, 4), (3, 4), (5, 3), (5, 0), (5, 2), (5, 4), (1, 5)),
)
SINGLE = (
    ((5, 0), (0, 6), (1, 6), (2, 7), (1, 7), (6, 0)),
    ((2, 0), (0, 6), (2, 6), (4, 6), (5, 7), (4, 7)),
)
KEPT = 6
HELD = len(MEMBERS[0])
AXES = ("blk", "team")
ROWS = 512
HALF = 256
FEAT = 128
UNROLL = 4
ROW_TOTAL = FEAT + 3

NEG_RATE = -math.sqrt(5.0) / math.log(2.0)
GAMMA = 1.0 / math.log(2.0)
SCALE = -(5.0 / 3.0) * math.log(2.0)

ROWS_BY_ROWS = (((1,), (1,)), ((), ()))
ROWS_BY_COLUMNS = (((1,), (0,)), ((), ()))


def device_at(x, y, z, core):
    return (((y % 4) * 2 + (z & 1)) * 2 + core) * 8 + ((z % 4) >> 1) * 4 + x % 4


def shift(moves, back=False):
    pairs = []
    for x, y, z, core in itertools.product(range(4), range(4), range(4), range(2)):
        dx, dy, dz = moves[core]
        here, there = device_at(x, y, z, core), device_at(x + dx, y + dy, z + dz, core)
        pairs.append((here, there) if back else (there, here))
    return pairs


def sibling():
    return [
        (device_at(x, y, z, core), device_at(x, y, z, 1 - core))
        for x, y, z, core in itertools.product(range(4), range(4), range(4), range(2))
    ]


def prepare(i, chunk_ref, left_x, right_x, left_v, right_v, turned):
    chunk = chunk_ref[...]
    rows = chunk.shape[0]
    x = chunk[:, :FEAT]
    wide = x.astype(jnp.float32)
    norm = jnp.sum(wide * wide, axis=1, keepdims=True)
    high = norm.astype(jnp.bfloat16).astype(jnp.float32)
    middle = (norm - high).astype(jnp.bfloat16).astype(jnp.float32)
    low = norm - high - middle
    lane = lax.broadcasted_iota(jnp.int32, (rows, FEAT), 1)
    parts = jnp.where(lane % 3 == 0, high, jnp.where(lane % 3 == 1, middle, low))
    left_x[i, :, :FEAT] = (wide * -2.0).astype(jnp.bfloat16)
    left_x[i, :, FEAT:] = jnp.where(lane < 3, 1.0, jnp.where(lane < 6, parts, 0.0)).astype(jnp.bfloat16)
    right_x[i, :, :FEAT] = x
    right_x[i, :, FEAT:] = jnp.where(lane < 3, parts, jnp.where(lane < 6, 1.0, 0.0)).astype(jnp.bfloat16)
    left_v[i] = chunk[:, FEAT:]
    right_v[i, :, :FEAT] = chunk[:, 2 * FEAT :]
    right_v[i, :, FEAT:] = chunk[:, FEAT : 2 * FEAT]
    turned[i, :FEAT, :] = wide.T.astype(jnp.bfloat16)
    row = lax.broadcasted_iota(jnp.int32, (16, rows), 0)
    turned[i, FEAT:, :] = jnp.where(row == ROW_TOTAL - FEAT, 1.0, 0.0).astype(jnp.bfloat16)


def pair_kernel(table, *refs):
    chunks = refs[:HELD]
    own_ref, others_ref = refs[HELD : HELD + 2]
    left_x, right_x, left_v, right_v, turned, total, total_turned = refs[HELD + 2 :]
    for i in range(HELD):
        prepare(i, chunks[i], left_x, right_x, left_v, right_v, turned)
    total[...] = jnp.zeros_like(total)
    total_turned[...] = jnp.zeros_like(total_turned)

    def meet(a, b, first, rows, both):
        strip = pl.ds(first, rows)
        dist_sq = lax.dot_general(
            left_x[a, strip, :], right_x[b], ROWS_BY_ROWS, preferred_element_type=jnp.float32
        )
        couple = lax.dot_general(
            left_v[a, strip, :], right_v[b], ROWS_BY_ROWS, preferred_element_type=jnp.float32
        )
        floor = jnp.maximum(dist_sq, 1e-30)
        u = floor * lax.rsqrt(floor) * NEG_RATE
        weight = ((GAMMA - u) * jnp.exp2(u) * couple).astype(jnp.bfloat16)
        total[a, strip, :] += lax.dot_general(
            weight, right_x[b], ROWS_BY_COLUMNS, preferred_element_type=jnp.float32
        )
        if both:
            total_turned[b] += lax.dot_general(
                turned[a, :, first : first + rows], weight, ROWS_BY_COLUMNS,
                preferred_element_type=jnp.float32,
            )

    def run(first_task, last_task, both):
        def one(s):
            meet(table[2 * s], table[2 * s + 1], 0, ROWS, both)

        looped = (last_task - first_task) // UNROLL * UNROLL

        @pl.loop(first_task, first_task + looped, step=UNROLL)
        def _(s):
            for k in range(UNROLL):
                one(s + k)

        for s in range(first_task + looped, last_task):
            one(s)

    run(0, len(BOTH[0]), True)
    run(len(BOTH[0]), len(BOTH[0]) + len(SINGLE[0]), False)
    meet(0, 0, 0, HALF, False)
    for i in range(KEPT):
        back = total_turned[i].T
        moved = total[i, :, :FEAT] + back[:, :FEAT]
        row_total = total[i, :, ROW_TOTAL : ROW_TOTAL + 1] + back[:, ROW_TOTAL : ROW_TOTAL + 1]
        grad = (row_total * right_x[i, :, :FEAT].astype(jnp.float32) - moved) * SCALE
        if i == 0:
            own_ref[...] = grad
        else:
            others_ref[i - 1] = grad.astype(others_ref.dtype)


def sums_over_pairs(table, chunks):
    whole = pl.BlockSpec(memory_space=pltpu.VMEM)
    stack = pltpu.VMEM((HELD, ROWS, 2 * FEAT), jnp.bfloat16)
    return pl.pallas_call(
        pair_kernel,
        out_shape=(
            jax.ShapeDtypeStruct((ROWS, FEAT), jnp.float32),
            jax.ShapeDtypeStruct((KEPT - 1, ROWS, FEAT), jnp.bfloat16),
        ),
        in_specs=[pl.BlockSpec(memory_space=pltpu.SMEM)] + [whole] * HELD,
        out_specs=(whole, whole),
        scratch_shapes=[stack] * 4
        + [
            pltpu.VMEM((HELD, FEAT + 16, ROWS), jnp.bfloat16),
            pltpu.VMEM((KEPT + 1, ROWS, 2 * FEAT), jnp.float32),
            pltpu.VMEM((KEPT, FEAT + 16, ROWS), jnp.float32),
        ],
        compiler_params=pltpu.CompilerParams(vmem_limit_bytes=48 * 1024 * 1024),
    )(table, *chunks)


def local(features, left_vectors, right_vectors):
    core = lax.axis_index("blk") % 2
    tables = np.array([BOTH[c] + SINGLE[c] for c in range(2)], np.int32).reshape(2, -1)
    table = jnp.where(core == 0, tables[0], tables[1])
    mine = jnp.concatenate([features, left_vectors, right_vectors], axis=1)
    chunk = jnp.concatenate([mine, lax.ppermute(mine, AXES, sibling())], axis=0)
    chunks = [chunk]
    for i in range(1, HELD):
        chunks.append(lax.ppermute(chunk, AXES, shift((MEMBERS[0][i], MEMBERS[1][i]))))
    own, others = sums_over_pairs(table, chunks)
    total = own
    for i in range(1, KEPT):
        back = lax.ppermute(others[i - 1], AXES, shift((MEMBERS[0][i], MEMBERS[1][i]), back=True))
        total = total + back.astype(jnp.float32)
    return total[:HALF] + lax.ppermute(total[HALF:], AXES, sibling())


def solution(mesh):
    spec = P(AXES, None)
    return jax.shard_map(
        local, mesh=mesh, in_specs=(spec, spec, spec), out_specs=spec, check_vma=False
    )
```

```python
import functools
import itertools
import math

import jax
import jax.numpy as jnp
import numpy as np
from jax import lax
from jax.experimental import pallas as pl
from jax.experimental.pallas import tpu as pltpu
from jax.sharding import PartitionSpec as P

MEMBERS = (
    ((0, 0, 0), (0, 3, 1), (0, 3, 3), (3, 0, 1), (1, 1, 0), (2, 0, 1), (0, 2, 3), (0, 0, 3)),
    ((0, 0, 0), (3, 3, 1), (3, 0, 1), (0, 2, 0), (0, 0, 3), (1, 2, 0), (0, 0, 2), (2, 0, 0)),
)
SOURCE = (0, 2, 0, 0, 0, 3, 2, 2)
KEPT = (0, 1, 2, 3, 4, 5)
STAGES = (
    (
        (((0, 4), (2, 0)), ((2, 3), (3, 2), (3, 4), (4, 3))),
        (((2, 0), (4, 3)), ((0, 3), (0, 4), (4, 0), (4, 2))),
    ),
    (
        (((0, 5), (1, 0), (1, 4), (1, 5), (2, 5), (3, 1), (5, 3)), ((2, 1), (4, 5), (5, 4))),
        (((0, 5), (1, 0), (1, 2), (1, 3), (1, 4), (4, 5), (5, 1)), ((2, 5), (5, 2))),
    ),
    (
        ((), ((1, 6), (1, 7), (3, 6), (3, 7), (4, 7), (5, 6), (5, 7))),
        ((), ((0, 7), (1, 6), (2, 6), (2, 7), (3, 6), (3, 7), (5, 6))),
    ),
)
ORDER = (2, 3, 4, 1, 5, 6, 7)
AXES = ("blk", "team")
HELD = len(MEMBERS[0])
ROWS = 512
HALF = 256
FEAT = 128
UNROLL = 4
ROW_TOTAL = FEAT + 3

NEG_RATE = -math.sqrt(5.0) / math.log(2.0)
GAMMA = 1.0 / math.log(2.0)
SCALE = -(5.0 / 3.0) * math.log(2.0)

ROWS_BY_ROWS = (((1,), (1,)), ((), ()))
ROWS_BY_COLUMNS = (((1,), (0,)), ((), ()))


def device_at(x, y, z, core):
    return (((y % 4) * 2 + (z & 1)) * 2 + core) * 8 + ((z % 4) >> 1) * 4 + x % 4


def shift(moves, back=False):
    pairs = []
    for x, y, z, core in itertools.product(range(4), range(4), range(4), range(2)):
        dx, dy, dz = moves[core]
        here, there = device_at(x, y, z, core), device_at(x + dx, y + dy, z + dz, core)
        pairs.append((here, there) if back else (there, here))
    return pairs


def sibling():
    return [
        (device_at(x, y, z, core), device_at(x, y, z, 1 - core))
        for x, y, z, core in itertools.product(range(4), range(4), range(4), range(2))
    ]


class Stage:
    def __init__(self, pairs, with_own):
        both = [pairs[c][0] for c in range(2)]
        single = [pairs[c][1] for c in range(2)]
        every = [p for c in range(2) for p in both[c] + single[c]]
        own = [(0, 0)] if with_own else []
        sums = {a for a, _ in every + own} | {b for c in range(2) for _, b in both[c]}
        used = sums | {b for _, b in every + own}
        self.sums = sorted(sums)
        self.ids = self.sums + sorted(used - sums)
        place = {i: n for n, i in enumerate(self.ids)}
        self.lefts = sorted({place[a] for a, _ in every + own})
        self.rights = sorted({place[b] for _, b in every + own})
        self.turns = sorted({place[a] for c in range(2) for a, _ in both[c]})
        spare = len(self.sums)
        self.slots = max(len(self.ids), spare + 1)
        self.count = [max(len(q[0]), len(q[1])) for q in (both, single)]
        self.with_own = with_own

        def padded(pairs, count):
            local = [(place[a], place[b]) for a, b in pairs]
            return local + [(spare, spare)] * (count - len(local))

        self.table = np.array(
            [padded(both[c], self.count[0]) + padded(single[c], self.count[1]) for c in range(2)],
            np.int32,
        ).reshape(2, -1)


def prepare(i, chunk_ref, stage, left_x, right_x, left_v, right_v, turned):
    chunk = chunk_ref[...]
    rows = chunk.shape[0]
    x = chunk[:, :FEAT]
    wide = x.astype(jnp.float32)
    norm = jnp.sum(wide * wide, axis=1, keepdims=True)
    high = norm.astype(jnp.bfloat16).astype(jnp.float32)
    middle = (norm - high).astype(jnp.bfloat16).astype(jnp.float32)
    low = norm - high - middle
    lane = lax.broadcasted_iota(jnp.int32, (rows, FEAT), 1)
    if i in stage.lefts:
        tail = jnp.where(lane == 3, high, jnp.where(lane == 4, middle, jnp.where(lane == 5, low, 0.0)))
        left_x[i, :, :FEAT] = (wide * -2.0).astype(jnp.bfloat16)
        left_x[i, :, FEAT:] = jnp.where(lane < 3, 1.0, tail).astype(jnp.bfloat16)
        left_v[i] = chunk[:, FEAT:]
    if i in stage.rights:
        tail = jnp.where(lane == 0, high, jnp.where(lane == 1, middle, jnp.where(lane == 2, low, 1.0)))
        right_x[i, :, :FEAT] = x
        right_x[i, :, FEAT:] = jnp.where(lane < 6, tail, 0.0).astype(jnp.bfloat16)
        right_v[i, :, :FEAT] = chunk[:, 2 * FEAT :]
        right_v[i, :, FEAT:] = chunk[:, FEAT : 2 * FEAT]
    if i in stage.turns:
        turned[i, :FEAT, :] = wide.T.astype(jnp.bfloat16)
        row = lax.broadcasted_iota(jnp.int32, (16, rows), 0)
        turned[i, FEAT:, :] = jnp.where(row == ROW_TOTAL - FEAT, 1.0, 0.0).astype(jnp.bfloat16)


def pair_kernel(stage, earlier, table, *refs):
    chunks, refs = refs[: len(stage.ids)], refs[len(stage.ids) :]
    before, refs = dict(zip(earlier, refs)), refs[len(earlier) :]
    out_refs, refs = refs[: len(stage.sums)], refs[len(stage.sums) :]
    left_x, right_x, left_v, right_v, turned, total, total_turned = refs
    for i in range(len(stage.ids)):
        prepare(i, chunks[i], stage, left_x, right_x, left_v, right_v, turned)
    total[...] = jnp.zeros_like(total)
    total_turned[...] = jnp.zeros_like(total_turned)

    def meet(a, b, rows, both):
        dist_sq = lax.dot_general(
            left_x[a, :rows, :], right_x[b], ROWS_BY_ROWS, preferred_element_type=jnp.float32
        )
        couple = lax.dot_general(
            left_v[a, :rows, :], right_v[b], ROWS_BY_ROWS, preferred_element_type=jnp.float32
        )
        floor = jnp.maximum(dist_sq, 1e-30)
        u = floor * lax.rsqrt(floor) * NEG_RATE
        weight = ((GAMMA - u) * jnp.exp2(u) * couple).astype(jnp.bfloat16)
        total[a, :rows, :] += lax.dot_general(
            weight, right_x[b], ROWS_BY_COLUMNS, preferred_element_type=jnp.float32
        )
        if both:
            total_turned[b] += lax.dot_general(
                turned[a], weight, ROWS_BY_COLUMNS, preferred_element_type=jnp.float32
            )

    def run(first_task, last_task, both):
        def one(s):
            meet(table[2 * s], table[2 * s + 1], ROWS, both)

        looped = (last_task - first_task) // UNROLL * UNROLL
        if looped > UNROLL:

            @pl.loop(first_task, first_task + looped, step=UNROLL)
            def _(s):
                for k in range(UNROLL):
                    one(s + k)

        else:
            looped = 0
        for s in range(first_task + looped, last_task):
            one(s)

    if stage.with_own:
        meet(0, 0, HALF, False)
    run(0, stage.count[0], True)
    run(stage.count[0], sum(stage.count), False)
    for i, out_ref in enumerate(out_refs):
        moved = total[i, :, :FEAT]
        row_total = total[i, :, ROW_TOTAL : ROW_TOTAL + 1]
        if stage.count[0]:
            back = total_turned[i].T
            moved = moved + back[:, :FEAT]
            row_total = row_total + back[:, ROW_TOTAL : ROW_TOTAL + 1]
        grad = (row_total * chunks[i][:, :FEAT].astype(jnp.float32) - moved) * SCALE
        if i in before:
            grad = grad + before[i][...]
        out_ref[...] = grad.astype(out_ref.dtype)


def sums_over_pairs(stage, table, chunks, before, kinds):
    whole = pl.BlockSpec(memory_space=pltpu.VMEM)
    stack = pltpu.VMEM((stage.slots, ROWS, 2 * FEAT), jnp.bfloat16)
    sums = len(stage.sums) + 1
    turned_sums = sums if stage.count[0] else 1
    pairs = (stage.count[0] + stage.count[1]) * ROWS * ROWS
    return pl.pallas_call(
        functools.partial(pair_kernel, stage, tuple(before)),
        out_shape=[jax.ShapeDtypeStruct((ROWS, FEAT), kind) for kind in kinds],
        in_specs=[pl.BlockSpec(memory_space=pltpu.SMEM)] + [whole] * (len(chunks) + len(before)),
        out_specs=[whole] * len(kinds),
        scratch_shapes=[stack] * 4
        + [
            pltpu.VMEM((stage.slots, FEAT + 16, ROWS), jnp.bfloat16),
            pltpu.VMEM((sums, ROWS, 2 * FEAT), jnp.float32),
            pltpu.VMEM((turned_sums, FEAT + 16, ROWS), jnp.float32),
        ],
        compiler_params=pltpu.CompilerParams(vmem_limit_bytes=40 * 1024 * 1024),
        cost_estimate=pl.CostEstimate(
            flops=pairs * 2048, bytes_accessed=len(chunks) * ROWS * FEAT * 6, transcendentals=2 * pairs
        ),
    )(table, *chunks, *before.values())


def local(features, left_vectors, right_vectors):
    core = lax.axis_index("blk") % 2
    mine = jnp.concatenate([features, left_vectors, right_vectors], axis=1)
    chunks = [jnp.concatenate([mine, lax.ppermute(mine, AXES, sibling())], axis=0)]
    chunks += [None] * (HELD - 1)
    for i in ORDER:
        moves = [
            tuple(m - n for m, n in zip(MEMBERS[c][i], MEMBERS[c][SOURCE[i]])) for c in range(2)
        ]
        chunks[i] = lax.ppermute(chunks[SOURCE[i]], AXES, shift(moves))
    stages = [Stage(pairs, n == 0) for n, pairs in enumerate(STAGES)]
    sums, own = {}, []
    for n, stage in enumerate(stages):
        table = jnp.where(core == 0, stage.table[0], stage.table[1])
        last = [not any(i in later.sums for later in stages[n + 1 :]) for i in stage.sums]
        kinds = [jnp.bfloat16 if i and done else jnp.float32 for i, done in zip(stage.sums, last)]
        before = {k: sums[i] for k, i in enumerate(stage.sums) if i and i in sums}
        out = sums_over_pairs(stage, table, [chunks[i] for i in stage.ids], before, kinds)
        for i, value in zip(stage.sums, out):
            if i:
                sums[i] = value
            else:
                own.append(value)
    total = functools.reduce(jnp.add, own)
    for i in sums:
        moves = (MEMBERS[0][i], MEMBERS[1][i])
        total = total + lax.ppermute(sums[i], AXES, shift(moves, back=True)).astype(jnp.float32)
    return total[:HALF] + lax.ppermute(total[HALF:], AXES, sibling())


def solution(mesh):
    spec = P(AXES, None)
    return jax.shard_map(
        local, mesh=mesh, in_specs=(spec, spec, spec), out_specs=spec, check_vma=False
    )
```

```python
import functools
import itertools
import math

import jax
import jax.numpy as jnp
import numpy as np
from jax import lax
from jax.experimental import pallas as pl
from jax.experimental.pallas import tpu as pltpu
from jax.sharding import PartitionSpec as P

MEMBERS = (
    ((0, 0, 0), (0, 3, 1), (0, 3, 3), (3, 0, 1), (1, 1, 0), (2, 0, 1), (0, 2, 3), (0, 0, 3)),
    ((0, 0, 0), (3, 3, 1), (3, 0, 1), (0, 2, 0), (0, 0, 3), (1, 2, 0), (0, 0, 2), (2, 0, 0)),
)
SOURCE = (0, 2, 0, 0, 0, 3, 2, 2)
STAGES = (
    (
        (((2, 0), (2, 4), (3, 2), (3, 4)), ((0, 4), (4, 0))),
        (((2, 0), (2, 3), (2, 4), (4, 0)), ((3, 0), (4, 3))),
    ),
    (
        (((1, 0), (1, 5), (2, 5), (3, 1), (5, 3)), ((1, 6), (1, 7), (3, 6), (4, 5), (4, 7), (5, 0), (5, 4), (5, 6), (5, 7))),
        (((0, 5), (1, 2), (1, 3), (1, 4), (5, 1)), ((1, 0), (1, 6), (2, 5), (2, 6), (2, 7), (3, 6), (3, 7), (5, 2), (5, 6))),
    ),
    (
        ((), ((0, 5), (0, 6))),
        ((), ((0, 1), (0, 6), (0, 7))),
    ),
)
ORDER = (2, 3, 4, 1, 5, 6, 7)
AXES = ("blk", "team")
HELD = len(MEMBERS[0])
ROWS = 512
HALF = 256
FEAT = 128
UNROLL = 4
ROW_TOTAL = FEAT + 3

NEG_RATE = -math.sqrt(5.0) / math.log(2.0)
GAMMA = 1.0 / math.log(2.0)
SCALE = -(5.0 / 3.0) * math.log(2.0)

ROWS_BY_ROWS = (((1,), (1,)), ((), ()))
ROWS_BY_COLUMNS = (((1,), (0,)), ((), ()))


def device_at(x, y, z, core):
    return (((y % 4) * 2 + (z & 1)) * 2 + core) * 8 + ((z % 4) >> 1) * 4 + x % 4


def shift(moves, back=False):
    pairs = []
    for x, y, z, core in itertools.product(range(4), range(4), range(4), range(2)):
        dx, dy, dz = moves[core]
        here, there = device_at(x, y, z, core), device_at(x + dx, y + dy, z + dz, core)
        pairs.append((here, there) if back else (there, here))
    return pairs


def sibling():
    return [
        (device_at(x, y, z, core), device_at(x, y, z, 1 - core))
        for x, y, z, core in itertools.product(range(4), range(4), range(4), range(2))
    ]


class Stage:
    def __init__(self, pairs, with_own):
        both = [pairs[c][0] for c in range(2)]
        single = [pairs[c][1] for c in range(2)]
        every = [p for c in range(2) for p in both[c] + single[c]]
        own = [(0, 0)] if with_own else []
        sums = {a for a, _ in every + own} | {b for c in range(2) for _, b in both[c]}
        used = sums | {b for _, b in every + own}
        self.sums = sorted(sums)
        self.ids = self.sums + sorted(used - sums)
        place = {i: n for n, i in enumerate(self.ids)}
        self.lefts = sorted({place[a] for a, _ in every + own})
        self.rights = sorted({place[b] for _, b in every + own})
        self.turns = sorted({place[a] for c in range(2) for a, _ in both[c]})
        spare = len(self.sums)
        self.slots = max(len(self.ids), spare + 1)
        self.count = [max(len(q[0]), len(q[1])) for q in (both, single)]
        self.with_own = with_own

        def padded(pairs, count):
            local = [(place[a], place[b]) for a, b in pairs]
            return local + [(spare, spare)] * (count - len(local))

        self.table = np.array(
            [padded(both[c], self.count[0]) + padded(single[c], self.count[1]) for c in range(2)],
            np.int32,
        ).reshape(2, -1)


def prepare(i, chunk_ref, stage, left_x, right_x, left_v, right_v, turned):
    chunk = chunk_ref[...]
    x = chunk[:, :FEAT]
    wide = x.astype(jnp.float32)
    norm = jnp.broadcast_to(jnp.sum(wide * wide, axis=1, keepdims=True), wide.shape)
    high = norm.astype(jnp.bfloat16).astype(jnp.float32)
    middle = (norm - high).astype(jnp.bfloat16).astype(jnp.float32)
    low = norm - high - middle
    lane = lax.broadcasted_iota(jnp.int32, wide.shape, 1)
    rows = wide.shape[0]
    if i in stage.lefts:
        tail = jnp.where(lane == 3, high, jnp.where(lane == 4, middle, jnp.where(lane == 5, low, 0.0)))
        left_x[i, :, :FEAT] = (wide * -2.0).astype(jnp.bfloat16)
        left_x[i, :, FEAT:] = jnp.where(lane < 3, 1.0, tail).astype(jnp.bfloat16)
        left_v[i] = chunk[:, FEAT:]
    if i in stage.rights:
        tail = jnp.where(lane == 0, high, jnp.where(lane == 1, middle, jnp.where(lane == 2, low, 1.0)))
        right_x[i, :, :FEAT] = x
        right_x[i, :, FEAT:] = jnp.where(lane < 6, tail, 0.0).astype(jnp.bfloat16)
        right_v[i, :, :FEAT] = chunk[:, 2 * FEAT :]
        right_v[i, :, FEAT:] = chunk[:, FEAT : 2 * FEAT]
    if i in stage.turns:
        turned[i, :FEAT, :] = wide.T.astype(jnp.bfloat16)
        row = lax.broadcasted_iota(jnp.int32, (16, rows), 0)
        turned[i, FEAT:, :] = jnp.where(row == ROW_TOTAL - FEAT, 1.0, 0.0).astype(jnp.bfloat16)


def pair_kernel(stage, earlier, table, *refs):
    chunks, refs = refs[: len(stage.ids)], refs[len(stage.ids) :]
    before, refs = dict(zip(earlier, refs)), refs[len(earlier) :]
    out_refs, refs = refs[: len(stage.sums)], refs[len(stage.sums) :]
    left_x, right_x, left_v, right_v, turned, total, total_turned = refs
    for i in range(len(stage.ids)):
        prepare(i, chunks[i], stage, left_x, right_x, left_v, right_v, turned)
    total[...] = jnp.zeros_like(total)
    total_turned[...] = jnp.zeros_like(total_turned)

    def meet(a, b, rows, both):
        dist_sq = lax.dot_general(
            left_x[a, :rows, :], right_x[b], ROWS_BY_ROWS, preferred_element_type=jnp.float32
        )
        couple = lax.dot_general(
            left_v[a, :rows, :], right_v[b], ROWS_BY_ROWS, preferred_element_type=jnp.float32
        )
        floor = jnp.maximum(dist_sq, 1e-30)
        u = floor * lax.rsqrt(floor) * NEG_RATE
        weight = ((GAMMA - u) * jnp.exp2(u) * couple).astype(jnp.bfloat16)
        total[a, :rows, :] += lax.dot_general(
            weight, right_x[b], ROWS_BY_COLUMNS, preferred_element_type=jnp.float32
        )
        if both:
            total_turned[b] += lax.dot_general(
                turned[a], weight, ROWS_BY_COLUMNS, preferred_element_type=jnp.float32
            )

    def run(first_task, last_task, both):
        def one(s):
            meet(table[2 * s], table[2 * s + 1], ROWS, both)

        looped = (last_task - first_task) // UNROLL * UNROLL
        if looped > UNROLL:

            @pl.loop(first_task, first_task + looped, step=UNROLL)
            def _(s):
                for k in range(UNROLL):
                    one(s + k)

        else:
            looped = 0
        for s in range(first_task + looped, last_task):
            one(s)

    if stage.with_own:
        meet(0, 0, HALF, False)
    run(0, stage.count[0], True)
    run(stage.count[0], sum(stage.count), False)
    for i, out_ref in enumerate(out_refs):
        moved = total[i, :, :FEAT]
        row_total = total[i, :, ROW_TOTAL : ROW_TOTAL + 1]
        if stage.count[0]:
            back = total_turned[i].T
            moved = moved + back[:, :FEAT]
            row_total = row_total + back[:, ROW_TOTAL : ROW_TOTAL + 1]
        grad = (row_total * chunks[i][:, :FEAT].astype(jnp.float32) - moved) * SCALE
        if i in before:
            grad = grad + before[i][...]
        out_ref[...] = grad.astype(out_ref.dtype)


def sums_over_pairs(stage, table, chunks, before, kinds):
    whole = pl.BlockSpec(memory_space=pltpu.VMEM)
    stack = pltpu.VMEM((stage.slots, ROWS, 2 * FEAT), jnp.bfloat16)
    sums = len(stage.sums) + 1
    turned_sums = sums if stage.count[0] else 1
    pairs = (stage.count[0] + stage.count[1]) * ROWS * ROWS
    return pl.pallas_call(
        functools.partial(pair_kernel, stage, tuple(before)),
        out_shape=[jax.ShapeDtypeStruct((ROWS, FEAT), kind) for kind in kinds],
        in_specs=[pl.BlockSpec(memory_space=pltpu.SMEM)] + [whole] * (len(chunks) + len(before)),
        out_specs=[whole] * len(kinds),
        scratch_shapes=[stack] * 4
        + [
            pltpu.VMEM((stage.slots, FEAT + 16, ROWS), jnp.bfloat16),
            pltpu.VMEM((sums, ROWS, 2 * FEAT), jnp.float32),
            pltpu.VMEM((turned_sums, FEAT + 16, ROWS), jnp.float32),
        ],
        compiler_params=pltpu.CompilerParams(vmem_limit_bytes=40 * 1024 * 1024),
        cost_estimate=pl.CostEstimate(
            flops=pairs * 2048, bytes_accessed=len(chunks) * ROWS * FEAT * 6, transcendentals=2 * pairs
        ),
    )(table, *chunks, *before.values())


def local(features, left_vectors, right_vectors):
    core = lax.axis_index("blk") % 2
    mine = jnp.concatenate([features, left_vectors, right_vectors], axis=1)
    chunks = [jnp.concatenate([mine, lax.ppermute(mine, AXES, sibling())], axis=0)]
    chunks += [None] * (HELD - 1)
    for i in ORDER:
        moves = [
            tuple(m - n for m, n in zip(MEMBERS[c][i], MEMBERS[c][SOURCE[i]])) for c in range(2)
        ]
        chunks[i] = lax.ppermute(chunks[SOURCE[i]], AXES, shift(moves))
    stages = [Stage(pairs, n == 0) for n, pairs in enumerate(STAGES)]
    sums, own = {}, []
    for n, stage in enumerate(stages):
        table = jnp.where(core == 0, stage.table[0], stage.table[1])
        last = [not any(i in later.sums for later in stages[n + 1 :]) for i in stage.sums]
        kinds = [jnp.bfloat16 if i and done else jnp.float32 for i, done in zip(stage.sums, last)]
        before = {k: sums[i] for k, i in enumerate(stage.sums) if i and i in sums}
        out = sums_over_pairs(stage, table, [chunks[i] for i in stage.ids], before, kinds)
        for i, value in zip(stage.sums, out):
            if i:
                sums[i] = value
            else:
                own.append(value)
    total = functools.reduce(jnp.add, own)
    for i in sums:
        moves = (MEMBERS[0][i], MEMBERS[1][i])
        total = total + lax.ppermute(sums[i], AXES, shift(moves, back=True)).astype(jnp.float32)
    return total[:HALF] + lax.ppermute(total[HALF:], AXES, sibling())


def solution(mesh):
    spec = P(AXES, None)
    return jax.shard_map(
        local, mesh=mesh, in_specs=(spec, spec, spec), out_specs=spec, check_vma=False
    )
```

```python
import functools
import itertools
import math

import jax
import jax.numpy as jnp
import numpy as np
from jax import lax
from jax.experimental import pallas as pl
from jax.experimental.pallas import tpu as pltpu
from jax.sharding import PartitionSpec as P

MEMBERS = (
    ((0, 0, 0), (0, 3, 1), (0, 3, 3), (3, 0, 1), (1, 1, 0), (2, 0, 1), (0, 2, 3), (0, 0, 3)),
    ((0, 0, 0), (3, 3, 1), (3, 0, 1), (0, 2, 0), (0, 0, 3), (1, 2, 0), (0, 0, 2), (2, 0, 0)),
)
SOURCE = (0, 2, 0, 0, 0, 3, 2, 2)
STAGES = (
    (
        (((2, 0), (2, 4), (3, 2), (3, 4)), ((0, 4), (4, 0))),
        (((2, 0), (2, 3), (2, 4), (4, 0)), ((3, 0), (4, 3))),
    ),
    (
        (((1, 0), (1, 5), (2, 5), (3, 1), (5, 3)), ((1, 6), (1, 7), (3, 6), (4, 5), (4, 7), (5, 0), (5, 4), (5, 6), (5, 7))),
        (((0, 5), (1, 2), (1, 3), (1, 4), (5, 1)), ((1, 0), (1, 6), (2, 5), (2, 6), (2, 7), (3, 6), (3, 7), (5, 2), (5, 6))),
    ),
    (
        ((), ((0, 5), (0, 6))),
        ((), ((0, 1), (0, 6), (0, 7))),
    ),
)
ORDER = (2, 3, 4, 1, 5, 6, 7)
AXES = ("blk", "team")
HELD = len(MEMBERS[0])
ROWS = 512
HALF = 256
FEAT = 128
UNROLL = 4
ROW_TOTAL = FEAT + 3

NEG_RATE = -math.sqrt(5.0) / math.log(2.0)
GAMMA = 1.0 / math.log(2.0)
SCALE = -(5.0 / 3.0) * math.log(2.0)

ROWS_BY_ROWS = (((1,), (1,)), ((), ()))
ROWS_BY_COLUMNS = (((1,), (0,)), ((), ()))


def device_at(x, y, z, core):
    return (((y % 4) * 2 + (z & 1)) * 2 + core) * 8 + ((z % 4) >> 1) * 4 + x % 4


def shift(moves, back=False):
    pairs = []
    for x, y, z, core in itertools.product(range(4), range(4), range(4), range(2)):
        dx, dy, dz = moves[core]
        here, there = device_at(x, y, z, core), device_at(x + dx, y + dy, z + dz, core)
        pairs.append((here, there) if back else (there, here))
    return pairs


def sibling():
    return [
        (device_at(x, y, z, core), device_at(x, y, z, 1 - core))
        for x, y, z, core in itertools.product(range(4), range(4), range(4), range(2))
    ]


class Stage:
    def __init__(self, pairs, with_own):
        both = [pairs[c][0] for c in range(2)]
        single = [pairs[c][1] for c in range(2)]
        every = [p for c in range(2) for p in both[c] + single[c]]
        own = [(0, 0)] if with_own else []
        sums = {a for a, _ in every + own} | {b for c in range(2) for _, b in both[c]}
        used = sums | {b for _, b in every + own}
        self.sums = sorted(sums)
        self.ids = self.sums + sorted(used - sums)
        place = {i: n for n, i in enumerate(self.ids)}
        self.lefts = sorted({place[a] for a, _ in every + own})
        self.rights = sorted({place[b] for _, b in every + own})
        self.turns = sorted({place[a] for c in range(2) for a, _ in both[c]})
        spare = len(self.sums)
        self.slots = max(len(self.ids), spare + 1)
        self.count = [max(len(q[0]), len(q[1])) for q in (both, single)]
        self.with_own = with_own

        def padded(pairs, count):
            local = [(place[a], place[b]) for a, b in pairs]
            return local + [(spare, spare)] * (count - len(local))

        self.table = np.array(
            [padded(both[c], self.count[0]) + padded(single[c], self.count[1]) for c in range(2)],
            np.int32,
        ).reshape(2, -1)


def prepare(i, chunk_ref, stage, left_x, right_x, left_v, right_v, turned):
    chunk = chunk_ref[...]
    x = chunk[:, :FEAT]
    wide = x.astype(jnp.float32)
    norm = jnp.broadcast_to(jnp.sum(wide * wide, axis=1, keepdims=True), wide.shape)
    high = norm.astype(jnp.bfloat16).astype(jnp.float32)
    middle = (norm - high).astype(jnp.bfloat16).astype(jnp.float32)
    low = norm - high - middle
    lane = lax.broadcasted_iota(jnp.int32, wide.shape, 1)
    rows = wide.shape[0]
    if i in stage.lefts:
        tail = jnp.where(lane == 3, high, jnp.where(lane == 4, middle, jnp.where(lane == 5, low, 0.0)))
        left_x[i, :, :FEAT] = (wide * -2.0).astype(jnp.bfloat16)
        left_x[i, :, FEAT:] = jnp.where(lane < 3, 1.0, tail).astype(jnp.bfloat16)
        left_v[i] = chunk[:, FEAT:]
    if i in stage.rights:
        tail = jnp.where(lane == 0, high, jnp.where(lane == 1, middle, jnp.where(lane == 2, low, 1.0)))
        right_x[i, :, :FEAT] = x
        right_x[i, :, FEAT:] = jnp.where(lane < 6, tail, 0.0).astype(jnp.bfloat16)
        right_v[i, :, :FEAT] = chunk[:, 2 * FEAT :]
        right_v[i, :, FEAT:] = chunk[:, FEAT : 2 * FEAT]
    if i in stage.turns:
        turned[i, :FEAT, :] = wide.T.astype(jnp.bfloat16)
        row = lax.broadcasted_iota(jnp.int32, (16, rows), 0)
        turned[i, FEAT:, :] = jnp.where(row == ROW_TOTAL - FEAT, 1.0, 0.0).astype(jnp.bfloat16)


def pair_kernel(stage, earlier, table, *refs):
    chunks, refs = refs[: len(stage.ids)], refs[len(stage.ids) :]
    before, refs = dict(zip(earlier, refs)), refs[len(earlier) :]
    out_refs, refs = refs[: len(stage.sums)], refs[len(stage.sums) :]
    left_x, right_x, left_v, right_v, turned, total, total_turned = refs
    for i in range(len(stage.ids)):
        prepare(i, chunks[i], stage, left_x, right_x, left_v, right_v, turned)
    total[...] = jnp.zeros_like(total)
    total_turned[...] = jnp.zeros_like(total_turned)

    def meet(a, b, rows, both):
        dist_sq = lax.dot_general(
            left_x[a, :rows, :], right_x[b], ROWS_BY_ROWS, preferred_element_type=jnp.float32
        )
        couple = lax.dot_general(
            left_v[a, :rows, :], right_v[b], ROWS_BY_ROWS, preferred_element_type=jnp.float32
        )
        floor = jnp.maximum(dist_sq, 1e-30)
        u = floor * lax.rsqrt(floor) * NEG_RATE
        weight = ((GAMMA - u) * jnp.exp2(u) * couple).astype(jnp.bfloat16)
        total[a, :rows, :] += lax.dot_general(
            weight, right_x[b], ROWS_BY_COLUMNS, preferred_element_type=jnp.float32
        )
        if both:
            total_turned[b] += lax.dot_general(
                turned[a], weight, ROWS_BY_COLUMNS, preferred_element_type=jnp.float32
            )

    def run(first_task, last_task, both):
        def one(s):
            meet(table[2 * s], table[2 * s + 1], ROWS, both)

        looped = (last_task - first_task) // UNROLL * UNROLL
        if looped > UNROLL:

            @pl.loop(first_task, first_task + looped, step=UNROLL)
            def _(s):
                for k in range(UNROLL):
                    one(s + k)

        else:
            looped = 0
        for s in range(first_task + looped, last_task):
            one(s)

    if stage.with_own:
        meet(0, 0, HALF, False)
    run(0, stage.count[0], True)
    run(stage.count[0], sum(stage.count), False)
    for i, out_ref in enumerate(out_refs):
        moved = total[i, :, :FEAT]
        row_total = total[i, :, ROW_TOTAL : ROW_TOTAL + 1]
        if stage.count[0]:
            back = total_turned[i].T
            moved = moved + back[:, :FEAT]
            row_total = row_total + back[:, ROW_TOTAL : ROW_TOTAL + 1]
        grad = (row_total * chunks[i][:, :FEAT].astype(jnp.float32) - moved) * SCALE
        if i in before:
            grad = grad + before[i][...]
        out_ref[...] = grad.astype(out_ref.dtype)


def side_by_side(x_ref, left_ref, right_ref, out_ref):
    for n, ref in enumerate((x_ref, left_ref, right_ref)):
        out_ref[:, n * FEAT : (n + 1) * FEAT] = ref[...]


def joined(x, left, right):
    whole = pl.BlockSpec(memory_space=pltpu.VMEM)
    return pl.pallas_call(
        side_by_side,
        out_shape=jax.ShapeDtypeStruct((x.shape[0], 3 * FEAT), x.dtype),
        in_specs=[whole] * 3,
        out_specs=whole,
    )(x, left, right)


def sums_over_pairs(stage, table, chunks, before, kinds):
    whole = pl.BlockSpec(memory_space=pltpu.VMEM)
    stack = pltpu.VMEM((stage.slots, ROWS, 2 * FEAT), jnp.bfloat16)
    sums = len(stage.sums) + 1
    turned_sums = sums if stage.count[0] else 1
    pairs = (stage.count[0] + stage.count[1]) * ROWS * ROWS
    return pl.pallas_call(
        functools.partial(pair_kernel, stage, tuple(before)),
        out_shape=[jax.ShapeDtypeStruct((ROWS, FEAT), kind) for kind in kinds],
        in_specs=[pl.BlockSpec(memory_space=pltpu.SMEM)] + [whole] * (len(chunks) + len(before)),
        out_specs=[whole] * len(kinds),
        scratch_shapes=[stack] * 4
        + [
            pltpu.VMEM((stage.slots, FEAT + 16, ROWS), jnp.bfloat16),
            pltpu.VMEM((sums, ROWS, 2 * FEAT), jnp.float32),
            pltpu.VMEM((turned_sums, FEAT + 16, ROWS), jnp.float32),
        ],
        compiler_params=pltpu.CompilerParams(vmem_limit_bytes=40 * 1024 * 1024),
        cost_estimate=pl.CostEstimate(
            flops=pairs * 2048, bytes_accessed=len(chunks) * ROWS * FEAT * 6, transcendentals=2 * pairs
        ),
    )(table, *chunks, *before.values())


def local(features, left_vectors, right_vectors):
    core = lax.axis_index("blk") % 2
    mine = joined(features, left_vectors, right_vectors)
    chunks = [jnp.concatenate([mine, lax.ppermute(mine, AXES, sibling())], axis=0)]
    chunks += [None] * (HELD - 1)
    for i in ORDER:
        moves = [
            tuple(m - n for m, n in zip(MEMBERS[c][i], MEMBERS[c][SOURCE[i]])) for c in range(2)
        ]
        chunks[i] = lax.ppermute(chunks[SOURCE[i]], AXES, shift(moves))
    stages = [Stage(pairs, n == 0) for n, pairs in enumerate(STAGES)]
    sums, own = {}, []
    for n, stage in enumerate(stages):
        table = jnp.where(core == 0, stage.table[0], stage.table[1])
        last = [not any(i in later.sums for later in stages[n + 1 :]) for i in stage.sums]
        kinds = [jnp.bfloat16 if i and done else jnp.float32 for i, done in zip(stage.sums, last)]
        before = {k: sums[i] for k, i in enumerate(stage.sums) if i and i in sums}
        out = sums_over_pairs(stage, table, [chunks[i] for i in stage.ids], before, kinds)
        for i, value in zip(stage.sums, out):
            if i:
                sums[i] = value
            else:
                own.append(value)
    total = functools.reduce(jnp.add, own)
    for i in sums:
        moves = (MEMBERS[0][i], MEMBERS[1][i])
        total = total + lax.ppermute(sums[i], AXES, shift(moves, back=True)).astype(jnp.float32)
    return total[:HALF] + lax.ppermute(total[HALF:], AXES, sibling())


def solution(mesh):
    spec = P(AXES, None)
    return jax.shard_map(
        local, mesh=mesh, in_specs=(spec, spec, spec), out_specs=spec, check_vma=False
    )
```

```python
import functools
import itertools
import math

import jax
import jax.numpy as jnp
import numpy as np
from jax import lax
from jax.experimental import pallas as pl
from jax.experimental.pallas import tpu as pltpu
from jax.sharding import PartitionSpec as P

MEMBERS = (
    ((0, 0, 0), (1, 3, 0), (3, 3, 0), (1, 0, 3), (0, 1, 1), (1, 0, 2), (3, 2, 0), (3, 0, 0)),
    ((0, 0, 0), (1, 3, 3), (1, 0, 3), (0, 2, 0), (3, 0, 0), (0, 2, 1), (2, 0, 0), (0, 0, 2)),
)
SOURCE = (0, 2, 0, 0, 0, 3, 2, 2)
STAGES = (
    (
        (((2, 0), (2, 4), (3, 2), (3, 4)), ((0, 4), (4, 0))),
        (((2, 0), (2, 3), (2, 4), (4, 0)), ((3, 0), (4, 3))),
    ),
    (
        (((1, 0), (1, 5), (2, 5), (3, 1), (5, 3)), ((1, 6), (1, 7), (3, 6), (4, 5), (4, 7), (5, 0), (5, 4), (5, 6), (5, 7))),
        (((0, 5), (1, 2), (1, 3), (1, 4), (5, 1)), ((1, 0), (1, 6), (2, 5), (2, 6), (2, 7), (3, 6), (3, 7), (5, 2), (5, 6))),
    ),
    (
        ((), ((0, 5), (0, 6))),
        ((), ((0, 1), (0, 6), (0, 7))),
    ),
)
ORDER = (2, 3, 4, 1, 5, 6, 7)
AXES = ("blk", "team")
HELD = len(MEMBERS[0])
ROWS = 512
HALF = 256
FEAT = 128
UNROLL = 4
ROW_TOTAL = FEAT + 3

NEG_RATE = -math.sqrt(5.0) / math.log(2.0)
GAMMA = 1.0 / math.log(2.0)
SCALE = -(5.0 / 3.0) * math.log(2.0)

ROWS_BY_ROWS = (((1,), (1,)), ((), ()))
ROWS_BY_COLUMNS = (((1,), (0,)), ((), ()))


def device_at(x, y, z, core):
    return (((y % 4) * 2 + (z & 1)) * 2 + core) * 8 + ((z % 4) >> 1) * 4 + x % 4


def shift(moves, back=False):
    pairs = []
    for x, y, z, core in itertools.product(range(4), range(4), range(4), range(2)):
        dx, dy, dz = moves[core]
        here, there = device_at(x, y, z, core), device_at(x + dx, y + dy, z + dz, core)
        pairs.append((here, there) if back else (there, here))
    return pairs


def sibling():
    return [
        (device_at(x, y, z, core), device_at(x, y, z, 1 - core))
        for x, y, z, core in itertools.product(range(4), range(4), range(4), range(2))
    ]


class Stage:
    def __init__(self, pairs, with_own):
        both = [pairs[c][0] for c in range(2)]
        single = [pairs[c][1] for c in range(2)]
        every = [p for c in range(2) for p in both[c] + single[c]]
        own = [(0, 0)] if with_own else []
        sums = {a for a, _ in every + own} | {b for c in range(2) for _, b in both[c]}
        used = sums | {b for _, b in every + own}
        self.sums = sorted(sums)
        self.ids = self.sums + sorted(used - sums)
        place = {i: n for n, i in enumerate(self.ids)}
        self.lefts = sorted({place[a] for a, _ in every + own})
        self.rights = sorted({place[b] for _, b in every + own})
        self.turns = sorted({place[a] for c in range(2) for a, _ in both[c]})
        spare = len(self.sums)
        self.slots = max(len(self.ids), spare + 1)
        self.count = [max(len(q[0]), len(q[1])) for q in (both, single)]
        self.with_own = with_own

        def padded(pairs, count):
            local = [(place[a], place[b]) for a, b in pairs]
            return local + [(spare, spare)] * (count - len(local))

        self.table = np.array(
            [padded(both[c], self.count[0]) + padded(single[c], self.count[1]) for c in range(2)],
            np.int32,
        ).reshape(2, -1)


def prepare(i, chunk_ref, stage, left_x, right_x, left_v, right_v, turned):
    chunk = chunk_ref[...]
    x = chunk[:, :FEAT]
    wide = x.astype(jnp.float32)
    norm = jnp.broadcast_to(jnp.sum(wide * wide, axis=1, keepdims=True), wide.shape)
    high = norm.astype(jnp.bfloat16).astype(jnp.float32)
    middle = (norm - high).astype(jnp.bfloat16).astype(jnp.float32)
    low = norm - high - middle
    lane = lax.broadcasted_iota(jnp.int32, wide.shape, 1)
    rows = wide.shape[0]
    if i in stage.lefts:
        tail = jnp.where(lane == 3, high, jnp.where(lane == 4, middle, jnp.where(lane == 5, low, 0.0)))
        left_x[i, :, :FEAT] = (wide * -2.0).astype(jnp.bfloat16)
        left_x[i, :, FEAT:] = jnp.where(lane < 3, 1.0, tail).astype(jnp.bfloat16)
        left_v[i] = chunk[:, FEAT:]
    if i in stage.rights:
        tail = jnp.where(lane == 0, high, jnp.where(lane == 1, middle, jnp.where(lane == 2, low, 1.0)))
        right_x[i, :, :FEAT] = x
        right_x[i, :, FEAT:] = jnp.where(lane < 6, tail, 0.0).astype(jnp.bfloat16)
        right_v[i, :, :FEAT] = chunk[:, 2 * FEAT :]
        right_v[i, :, FEAT:] = chunk[:, FEAT : 2 * FEAT]
    if i in stage.turns:
        turned[i, :FEAT, :] = wide.T.astype(jnp.bfloat16)
        row = lax.broadcasted_iota(jnp.int32, (16, rows), 0)
        turned[i, FEAT:, :] = jnp.where(row == ROW_TOTAL - FEAT, 1.0, 0.0).astype(jnp.bfloat16)


def pair_kernel(stage, earlier, table, *refs):
    chunks, refs = refs[: len(stage.ids)], refs[len(stage.ids) :]
    before, refs = dict(zip(earlier, refs)), refs[len(earlier) :]
    out_refs, refs = refs[: len(stage.sums)], refs[len(stage.sums) :]
    left_x, right_x, left_v, right_v, turned, total, total_turned = refs
    for i in range(len(stage.ids)):
        prepare(i, chunks[i], stage, left_x, right_x, left_v, right_v, turned)
    total[...] = jnp.zeros_like(total)
    total_turned[...] = jnp.zeros_like(total_turned)

    def meet(a, b, rows, both):
        dist_sq = lax.dot_general(
            left_x[a, :rows, :], right_x[b], ROWS_BY_ROWS, preferred_element_type=jnp.float32
        )
        couple = lax.dot_general(
            left_v[a, :rows, :], right_v[b], ROWS_BY_ROWS, preferred_element_type=jnp.float32
        )
        floor = jnp.maximum(dist_sq, 1e-30)
        u = floor * lax.rsqrt(floor) * NEG_RATE
        weight = ((GAMMA - u) * jnp.exp2(u) * couple).astype(jnp.bfloat16)
        total[a, :rows, :] += lax.dot_general(
            weight, right_x[b], ROWS_BY_COLUMNS, preferred_element_type=jnp.float32
        )
        if both:
            total_turned[b] += lax.dot_general(
                turned[a], weight, ROWS_BY_COLUMNS, preferred_element_type=jnp.float32
            )

    def run(first_task, last_task, both):
        def one(s):
            meet(table[2 * s], table[2 * s + 1], ROWS, both)

        looped = (last_task - first_task) // UNROLL * UNROLL
        if looped > UNROLL:

            @pl.loop(first_task, first_task + looped, step=UNROLL)
            def _(s):
                for k in range(UNROLL):
                    one(s + k)

        else:
            looped = 0
        for s in range(first_task + looped, last_task):
            one(s)

    if stage.with_own:
        meet(0, 0, HALF, False)
    run(0, stage.count[0], True)
    run(stage.count[0], sum(stage.count), False)
    for i, out_ref in enumerate(out_refs):
        moved = total[i, :, :FEAT]
        row_total = total[i, :, ROW_TOTAL : ROW_TOTAL + 1]
        if stage.count[0]:
            back = total_turned[i].T
            moved = moved + back[:, :FEAT]
            row_total = row_total + back[:, ROW_TOTAL : ROW_TOTAL + 1]
        grad = (row_total * chunks[i][:, :FEAT].astype(jnp.float32) - moved) * SCALE
        if i in before:
            grad = grad + before[i][...]
        out_ref[...] = grad.astype(out_ref.dtype)


def sums_over_pairs(stage, table, chunks, before, kinds):
    whole = pl.BlockSpec(memory_space=pltpu.VMEM)
    stack = pltpu.VMEM((stage.slots, ROWS, 2 * FEAT), jnp.bfloat16)
    sums = len(stage.sums) + 1
    turned_sums = sums if stage.count[0] else 1
    pairs = (stage.count[0] + stage.count[1]) * ROWS * ROWS
    return pl.pallas_call(
        functools.partial(pair_kernel, stage, tuple(before)),
        out_shape=[jax.ShapeDtypeStruct((ROWS, FEAT), kind) for kind in kinds],
        in_specs=[pl.BlockSpec(memory_space=pltpu.SMEM)] + [whole] * (len(chunks) + len(before)),
        out_specs=[whole] * len(kinds),
        scratch_shapes=[stack] * 4
        + [
            pltpu.VMEM((stage.slots, FEAT + 16, ROWS), jnp.bfloat16),
            pltpu.VMEM((sums, ROWS, 2 * FEAT), jnp.float32),
            pltpu.VMEM((turned_sums, FEAT + 16, ROWS), jnp.float32),
        ],
        compiler_params=pltpu.CompilerParams(vmem_limit_bytes=40 * 1024 * 1024),
        cost_estimate=pl.CostEstimate(
            flops=pairs * 2048, bytes_accessed=len(chunks) * ROWS * FEAT * 6, transcendentals=2 * pairs
        ),
    )(table, *chunks, *before.values())


def local(features, left_vectors, right_vectors):
    core = lax.axis_index("blk") % 2
    mine = jnp.concatenate([features, left_vectors, right_vectors], axis=1)
    chunks = [jnp.concatenate([mine, lax.ppermute(mine, AXES, sibling())], axis=0)]
    chunks += [None] * (HELD - 1)
    for i in ORDER:
        moves = [
            tuple(m - n for m, n in zip(MEMBERS[c][i], MEMBERS[c][SOURCE[i]])) for c in range(2)
        ]
        chunks[i] = lax.ppermute(chunks[SOURCE[i]], AXES, shift(moves))
    stages = [Stage(pairs, n == 0) for n, pairs in enumerate(STAGES)]
    sums, own = {}, []
    for n, stage in enumerate(stages):
        table = jnp.where(core == 0, stage.table[0], stage.table[1])
        last = [not any(i in later.sums for later in stages[n + 1 :]) for i in stage.sums]
        kinds = [jnp.bfloat16 if i and done else jnp.float32 for i, done in zip(stage.sums, last)]
        before = {k: sums[i] for k, i in enumerate(stage.sums) if i and i in sums}
        out = sums_over_pairs(stage, table, [chunks[i] for i in stage.ids], before, kinds)
        for i, value in zip(stage.sums, out):
            if i:
                sums[i] = value
            else:
                own.append(value)
    total = functools.reduce(jnp.add, own)
    for i in sums:
        moves = (MEMBERS[0][i], MEMBERS[1][i])
        total = total + lax.ppermute(sums[i], AXES, shift(moves, back=True)).astype(jnp.float32)
    return total[:HALF] + lax.ppermute(total[HALF:], AXES, sibling())


def solution(mesh):
    spec = P(AXES, None)
    return jax.shard_map(
        local, mesh=mesh, in_specs=(spec, spec, spec), out_specs=spec, check_vma=False
    )
```

```python
import functools
import itertools
import math

import jax
import jax.numpy as jnp
import numpy as np
from jax import lax
from jax.experimental import pallas as pl
from jax.experimental.pallas import tpu as pltpu
from jax.sharding import PartitionSpec as P

MEMBERS = (
    ((0, 0, 0), (0, 3, 1), (0, 3, 3), (3, 0, 1), (1, 1, 0), (2, 0, 1), (0, 2, 3), (0, 0, 3)),
    ((0, 0, 0), (3, 3, 1), (3, 0, 1), (0, 2, 0), (0, 0, 3), (1, 2, 0), (0, 0, 2), (2, 0, 0)),
)
SOURCE = (0, 2, 0, 0, 0, 3, 2, 2)
STAGES = (
    (
        (((2, 0), (2, 4), (3, 2), (3, 4)), ((0, 4), (4, 0))),
        (((2, 0), (2, 3), (2, 4), (4, 0)), ((3, 0), (4, 3))),
    ),
    (
        (((1, 0), (1, 5), (2, 5), (3, 1), (5, 3)), ((1, 6), (1, 7), (3, 6), (4, 5), (4, 7), (5, 0), (5, 4), (5, 6), (5, 7))),
        (((0, 5), (1, 2), (1, 3), (1, 4), (5, 1)), ((1, 0), (1, 6), (2, 5), (2, 6), (2, 7), (3, 6), (3, 7), (5, 2), (5, 6))),
    ),
    (
        ((), ((0, 5), (0, 6))),
        ((), ((0, 1), (0, 6), (0, 7))),
    ),
)
ORDER = (2, 3, 4, 1, 5, 6, 7)
AXES = ("blk", "team")
HELD = len(MEMBERS[0])
ROWS = 512
HALF = 256
FEAT = 128
UNROLL = 3
ROW_TOTAL = FEAT + 3

NEG_RATE = -math.sqrt(5.0) / math.log(2.0)
GAMMA = 1.0 / math.log(2.0)
SCALE = -(5.0 / 3.0) * math.log(2.0)

ROWS_BY_ROWS = (((1,), (1,)), ((), ()))
ROWS_BY_COLUMNS = (((1,), (0,)), ((), ()))


def device_at(x, y, z, core):
    return (((y % 4) * 2 + (z & 1)) * 2 + core) * 8 + ((z % 4) >> 1) * 4 + x % 4


def shift(moves, back=False):
    pairs = []
    for x, y, z, core in itertools.product(range(4), range(4), range(4), range(2)):
        dx, dy, dz = moves[core]
        here, there = device_at(x, y, z, core), device_at(x + dx, y + dy, z + dz, core)
        pairs.append((here, there) if back else (there, here))
    return pairs


def sibling():
    return [
        (device_at(x, y, z, core), device_at(x, y, z, 1 - core))
        for x, y, z, core in itertools.product(range(4), range(4), range(4), range(2))
    ]


class Stage:
    def __init__(self, pairs, with_own):
        both = [pairs[c][0] for c in range(2)]
        single = [pairs[c][1] for c in range(2)]
        every = [p for c in range(2) for p in both[c] + single[c]]
        own = [(0, 0)] if with_own else []
        sums = {a for a, _ in every + own} | {b for c in range(2) for _, b in both[c]}
        used = sums | {b for _, b in every + own}
        self.sums = sorted(sums)
        self.ids = self.sums + sorted(used - sums)
        place = {i: n for n, i in enumerate(self.ids)}
        self.lefts = sorted({place[a] for a, _ in every + own})
        self.rights = sorted({place[b] for _, b in every + own})
        self.turns = sorted({place[a] for c in range(2) for a, _ in both[c]})
        spare = len(self.sums)
        self.slots = max(len(self.ids), spare + 1)
        self.count = [max(len(q[0]), len(q[1])) for q in (both, single)]
        self.with_own = with_own

        def padded(pairs, count):
            local = [(place[a], place[b]) for a, b in pairs]
            return local + [(spare, spare)] * (count - len(local))

        self.table = np.array(
            [padded(both[c], self.count[0]) + padded(single[c], self.count[1]) for c in range(2)],
            np.int32,
        ).reshape(2, -1)


def prepare(i, chunk_ref, stage, left_x, right_x, left_v, right_v, turned):
    chunk = chunk_ref[...]
    x = chunk[:, :FEAT]
    wide = x.astype(jnp.float32)
    norm = jnp.broadcast_to(jnp.sum(wide * wide, axis=1, keepdims=True), wide.shape)
    high = norm.astype(jnp.bfloat16).astype(jnp.float32)
    middle = (norm - high).astype(jnp.bfloat16).astype(jnp.float32)
    low = norm - high - middle
    lane = lax.broadcasted_iota(jnp.int32, wide.shape, 1)
    rows = wide.shape[0]
    if i in stage.lefts:
        tail = jnp.where(lane == 3, high, jnp.where(lane == 4, middle, jnp.where(lane == 5, low, 0.0)))
        left_x[i, :, :FEAT] = (wide * -2.0).astype(jnp.bfloat16)
        left_x[i, :, FEAT:] = jnp.where(lane < 3, 1.0, tail).astype(jnp.bfloat16)
        left_v[i] = chunk[:, FEAT:]
    if i in stage.rights:
        tail = jnp.where(lane == 0, high, jnp.where(lane == 1, middle, jnp.where(lane == 2, low, 1.0)))
        right_x[i, :, :FEAT] = x
        right_x[i, :, FEAT:] = jnp.where(lane < 6, tail, 0.0).astype(jnp.bfloat16)
        right_v[i, :, :FEAT] = chunk[:, 2 * FEAT :]
        right_v[i, :, FEAT:] = chunk[:, FEAT : 2 * FEAT]
    if i in stage.turns:
        turned[i, :FEAT, :] = wide.T.astype(jnp.bfloat16)
        row = lax.broadcasted_iota(jnp.int32, (16, rows), 0)
        turned[i, FEAT:, :] = jnp.where(row == ROW_TOTAL - FEAT, 1.0, 0.0).astype(jnp.bfloat16)


def pair_kernel(stage, earlier, table, *refs):
    chunks, refs = refs[: len(stage.ids)], refs[len(stage.ids) :]
    before, refs = dict(zip(earlier, refs)), refs[len(earlier) :]
    out_refs, refs = refs[: len(stage.sums)], refs[len(stage.sums) :]
    left_x, right_x, left_v, right_v, turned, total, total_turned = refs
    for i in range(len(stage.ids)):
        prepare(i, chunks[i], stage, left_x, right_x, left_v, right_v, turned)
    for i in range(len(stage.sums)):
        total[i] = jnp.zeros(total.shape[1:], total.dtype)
        if stage.count[0]:
            total_turned[i] = jnp.zeros(total_turned.shape[1:], total_turned.dtype)

    def meet(a, b, rows, both):
        dist_sq = lax.dot_general(
            left_x[a, :rows, :], right_x[b], ROWS_BY_ROWS, preferred_element_type=jnp.float32
        )
        couple = lax.dot_general(
            left_v[a, :rows, :], right_v[b], ROWS_BY_ROWS, preferred_element_type=jnp.float32
        )
        floor = jnp.maximum(dist_sq, 1e-30)
        u = floor * lax.rsqrt(floor) * NEG_RATE
        weight = ((GAMMA - u) * jnp.exp2(u) * couple).astype(jnp.bfloat16)
        total[a, :rows, :] += lax.dot_general(
            weight, right_x[b], ROWS_BY_COLUMNS, preferred_element_type=jnp.float32
        )
        if both:
            total_turned[b] += lax.dot_general(
                turned[a], weight, ROWS_BY_COLUMNS, preferred_element_type=jnp.float32
            )

    def run(first_task, last_task, both):
        def one(s):
            meet(table[2 * s], table[2 * s + 1], ROWS, both)

        looped = (last_task - first_task) // UNROLL * UNROLL
        if looped > UNROLL:

            @pl.loop(first_task, first_task + looped, step=UNROLL)
            def _(s):
                for k in range(UNROLL):
                    one(s + k)

        else:
            looped = 0
        for s in range(first_task + looped, last_task):
            one(s)

    if stage.with_own:
        meet(0, 0, HALF, False)
    run(0, stage.count[0], True)
    run(stage.count[0], sum(stage.count), False)
    for i, out_ref in enumerate(out_refs):
        moved = total[i, :, :FEAT]
        row_total = total[i, :, ROW_TOTAL : ROW_TOTAL + 1]
        if stage.count[0]:
            back = total_turned[i].T
            moved = moved + back[:, :FEAT]
            row_total = row_total + back[:, ROW_TOTAL : ROW_TOTAL + 1]
        grad = (row_total * chunks[i][:, :FEAT].astype(jnp.float32) - moved) * SCALE
        if i in before:
            grad = grad + before[i][...]
        out_ref[...] = grad.astype(out_ref.dtype)


def sums_over_pairs(stage, table, chunks, before, kinds):
    whole = pl.BlockSpec(memory_space=pltpu.VMEM)
    stack = pltpu.VMEM((stage.slots, ROWS, 2 * FEAT), jnp.bfloat16)
    sums = len(stage.sums) + 1
    turned_sums = sums if stage.count[0] else 1
    pairs = (stage.count[0] + stage.count[1]) * ROWS * ROWS
    return pl.pallas_call(
        functools.partial(pair_kernel, stage, tuple(before)),
        out_shape=[jax.ShapeDtypeStruct((ROWS, FEAT), kind) for kind in kinds],
        in_specs=[pl.BlockSpec(memory_space=pltpu.SMEM)] + [whole] * (len(chunks) + len(before)),
        out_specs=[whole] * len(kinds),
        scratch_shapes=[stack] * 4
        + [
            pltpu.VMEM((stage.slots, FEAT + 16, ROWS), jnp.bfloat16),
            pltpu.VMEM((sums, ROWS, 2 * FEAT), jnp.float32),
            pltpu.VMEM((turned_sums, FEAT + 16, ROWS), jnp.float32),
        ],
        compiler_params=pltpu.CompilerParams(vmem_limit_bytes=40 * 1024 * 1024),
        cost_estimate=pl.CostEstimate(
            flops=pairs * 2048, bytes_accessed=len(chunks) * ROWS * FEAT * 6, transcendentals=2 * pairs
        ),
    )(table, *chunks, *before.values())


def local(features, left_vectors, right_vectors):
    core = lax.axis_index("blk") % 2
    mine = jnp.concatenate([features, left_vectors, right_vectors], axis=1)
    chunks = [jnp.concatenate([mine, lax.ppermute(mine, AXES, sibling())], axis=0)]
    chunks += [None] * (HELD - 1)
    for i in ORDER:
        moves = [
            tuple(m - n for m, n in zip(MEMBERS[c][i], MEMBERS[c][SOURCE[i]])) for c in range(2)
        ]
        chunks[i] = lax.ppermute(chunks[SOURCE[i]], AXES, shift(moves))
    stages = [Stage(pairs, n == 0) for n, pairs in enumerate(STAGES)]
    sums, own = {}, []
    for n, stage in enumerate(stages):
        table = jnp.where(core == 0, stage.table[0], stage.table[1])
        last = [not any(i in later.sums for later in stages[n + 1 :]) for i in stage.sums]
        kinds = [jnp.bfloat16 if i and done else jnp.float32 for i, done in zip(stage.sums, last)]
        before = {k: sums[i] for k, i in enumerate(stage.sums) if i and i in sums}
        out = sums_over_pairs(stage, table, [chunks[i] for i in stage.ids], before, kinds)
        for i, value in zip(stage.sums, out):
            if i:
                sums[i] = value
            else:
                own.append(value)
    total = functools.reduce(jnp.add, own)
    for i in sums:
        moves = (MEMBERS[0][i], MEMBERS[1][i])
        total = total + lax.ppermute(sums[i], AXES, shift(moves, back=True)).astype(jnp.float32)
    return total[:HALF] + lax.ppermute(total[HALF:], AXES, sibling())


def solution(mesh):
    spec = P(AXES, None)
    return jax.shard_map(
        local, mesh=mesh, in_specs=(spec, spec, spec), out_specs=spec, check_vma=False
    )
```
